32 devices in a mesh: ctx: 8 (over z, x), head: 4 (over y, core).
Axes of the slice: x: 2, y: 2, z: 4, core: 2. Of those that a mesh axis runs over, the one named last changes fastest.
Arguments:
- query_raw: bfloat16 [8192, 2048], P('ctx', 'head'), may hold values from -6 to 6
- key_raw: bfloat16 [8192, 2048], P('ctx', 'head'), may hold values from -6 to 6
- value_raw: bfloat16 [8192, 4096], P('ctx', 'head'), may hold values from -6 to 6
- gate_branch: bfloat16 [8192, 4096], P('ctx', 'head'), may hold values from -6 to 6
- gate_code: int32 [8192, 32], P('ctx', 'head'), may hold values from 0 to 1000
- beta_code: int32 [8192, 32], P('ctx', 'head'), may hold values from 0 to 1000
- conv_query: bfloat16 [4, 2048], P(None, 'head'), may hold values from -3 to 3
- conv_key: bfloat16 [4, 2048], P(None, 'head'), may hold values from -3 to 3
- conv_value: bfloat16 [4, 4096], P(None, 'head'), may hold values from -3 to 3
- norm_gain: float32 [128], replicated, may hold values from 0.1 to 1.9
- out_weight: bfloat16 [4096, 2048], P('head'), may hold values from -0.09375 to 0.09375
Outputs:
- layer_out: bfloat16 [8192, 2048], P(('ctx', 'head'))
The draws below stay inside these ranges and needn't reach their ends.
All inputs are finite; a program needn't handle non-finite values.
Results may differ from the reference program's by a relative error of at most 0.002.
The reference program's roundings to bfloat16 on the way count: a program that leaves them out, or rounds other values in their place, can miss the bound.
Values may be sent and summed in bfloat16 or wider, within the bound.
A program may use at most 128 MiB of HBM per device.

```python
import jax
import jax.numpy as jnp
from jax import lax

D = 2048
KEY_HEADS = 16
VALUE_HEADS = 32
HEAD_DIM = 128
KERNEL = 4
BLOCK = 64
TOKENS = 8192


def draw_gate_code(key, part):
    level_key = jax.random.fold_in(key, 11)
    order_key = jax.random.fold_in(key, 12)
    token_key = jax.random.fold_in(key, 13)
    ceilings = jax.random.randint(level_key, (VALUE_HEADS,), 0, 1001)
    order = jax.random.permutation(order_key, VALUE_HEADS)
    ceilings = ceilings.at[order[0]].set(1000)
    codes = jax.random.randint(token_key, (TOKENS, VALUE_HEADS), 0, ceilings[None, :] + 1)
    codes = codes.at[0, order[0]].set(1000)
    codes = codes.at[1, order[1]].set(0)
    return codes.astype(jnp.int32)


def plant(array, own_key, smallest, high):
    longest = array.shape.index(max(array.shape))
    spots = []
    for shift in (0, 1):
        where = [jax.random.randint(jax.random.fold_in(own_key, axis), (), 0, length) for axis, length in enumerate(array.shape)]
        where[longest] = (where[longest] + shift) % array.shape[longest]
        spots.append(tuple(where))
    return array.at[spots[0]].set(smallest).at[spots[1]].set(high)


def block_scale(rng, extent, cuts, smallest, top_value):
    factor_of, own = 1.0, jax.random.fold_in(rng, 6)
    for position, parts in cuts:
        heights = jnp.exp(jax.random.uniform(jax.random.fold_in(own, position), (parts,), jnp.float32, smallest / len(cuts), top_value / len(cuts)))
        factor_of = factor_of * jnp.repeat(heights, extent[position] // parts).reshape([-1 if axis == position else 1 for axis in range(len(extent))])
    return factor_of


def centred(own_key, shape, spread, limit, cuts=(), kind=jnp.bfloat16):
    level = block_scale(own_key, shape, cuts, -0.22, 0.18) if cuts else 1.0
    values = jax.random.normal(own_key, shape, jnp.float32) * spread * level
    return jnp.minimum(jnp.maximum(values, -limit), limit).astype(kind)


def setup_inputs(seed: int = 0) -> dict:
    key_of = jax.random.split(jax.random.key(seed), 12)
    return {
        "query_raw": centred(key_of[0], (TOKENS, KEY_HEADS * HEAD_DIM), 1.0, 6.0, ((0, 8), (1, 4))),
        "key_raw": centred(key_of[1], (TOKENS, KEY_HEADS * HEAD_DIM), 1.0, 6.0, ((0, 8), (1, 4))),
        "value_raw": centred(key_of[2], (TOKENS, VALUE_HEADS * HEAD_DIM), 1.0, 6.0, ((0, 8), (1, 4))),
        "gate_branch": centred(key_of[3], (TOKENS, VALUE_HEADS * HEAD_DIM), 1.0, 6.0, ((0, 8), (1, 4))),
        "gate_code": draw_gate_code(jax.random.fold_in(key_of[11], 71), 0),
        "beta_code": plant(jax.random.randint(key_of[5], (TOKENS, VALUE_HEADS), 0, 1001), jax.random.fold_in(key_of[5], 1), 0, 1000).astype(jnp.int32),
        "conv_query": centred(key_of[6], (KERNEL, KEY_HEADS * HEAD_DIM), KERNEL ** -0.5, 3.0, ((1, 4),)),
        "conv_key": centred(key_of[7], (KERNEL, KEY_HEADS * HEAD_DIM), KERNEL ** -0.5, 3.0, ((1, 4),)),
        "conv_value": centred(key_of[8], (KERNEL, VALUE_HEADS * HEAD_DIM), KERNEL ** -0.5, 3.0, ((1, 4),)),
        "norm_gain": jnp.clip(1.0 + 0.18 * jax.random.normal(key_of[9], (HEAD_DIM,), jnp.float32), 0.1, 1.9),
        "out_weight": centred(key_of[10], (VALUE_HEADS * HEAD_DIM, D), (VALUE_HEADS * HEAD_DIM) ** -0.5, 0.09375, ((0, 4),)),
    }


EXACT = lax.Precision.HIGHEST

def causal_conv(earlier, current, weights):
    length = current.shape[0]
    extended = jnp.concatenate([earlier, current], 0).astype(jnp.float32)
    running = jnp.zeros(current.shape, jnp.float32)
    for offset in range(KERNEL):
        running = running + weights[offset].astype(jnp.float32) * extended[offset:offset + length]
    return jax.nn.silu(running)

def unit_rows(values):
    return values * lax.rsqrt(lax.optimization_barrier(jnp.sum(values * values, -1, keepdims=True)) + 1e-06)

def neumann_inverse(strict_part):
    length = strict_part.shape[-1]
    identity = jnp.eye(length, dtype=jnp.float32)
    result = identity - strict_part
    powered = strict_part
    covered = 2
    while covered < length:
        powered = jnp.matmul(powered, powered, precision=EXACT)
        result = jnp.matmul(result, identity + powered, precision=EXACT)
        covered = covered * 2
    return result

def prepare(queries, key_rows, value_rows, log_gate, strength):
    length = queries.shape[-2]
    cumulated = jnp.cumsum(log_gate, axis=-1)
    gap_log = cumulated[..., :, None] - cumulated[..., None, :]
    row_ids = lax.broadcasted_iota(jnp.int32, (length, length), 0)
    col_ids = lax.broadcasted_iota(jnp.int32, (length, length), 1)
    causal_mask = row_ids >= col_ids
    strict_mask = row_ids > col_ids
    decays = jnp.exp(jnp.where(causal_mask, gap_log, 0.0))
    key_dots = jnp.einsum('...id,...jd->...ij', key_rows, key_rows, precision=EXACT)
    strict_part = jnp.where(strict_mask, strength[..., :, None] * key_dots * decays, 0.0)
    inverse = neumann_inverse(strict_part)
    gammas = jnp.exp(cumulated)
    wy_keys = jnp.einsum('...ij,...jd->...id', inverse, (strength * gammas)[..., None] * key_rows, precision=EXACT)
    wy_values = jnp.einsum('...ij,...jd->...id', inverse, strength[..., None] * value_rows, precision=EXACT)
    query_dots = jnp.einsum('...id,...jd->...ij', queries, key_rows, precision=EXACT)
    mixing = jnp.where(causal_mask, query_dots * decays, 0.0)
    key_tails = jnp.exp(cumulated[..., -1:] - cumulated)[..., None] * key_rows
    block_decay = jnp.exp(cumulated[..., -1])
    return (gammas, mixing, wy_keys, wy_values, key_tails, block_decay)

def gated_norm(emitted, branch, gain_vector):
    scaled = emitted * lax.rsqrt(lax.optimization_barrier(jnp.mean(emitted * emitted, -1, keepdims=True)) + 1e-06) * gain_vector
    gating = jax.nn.silu(branch.astype(jnp.float32)).reshape(emitted.shape)
    return (scaled * gating).reshape(emitted.shape[0], -1).astype(jnp.bfloat16)

def reference(query_raw, key_raw, value_raw, gate_branch, gate_code, beta_code, conv_query, conv_key, conv_value, norm_gain, out_weight):
    group_ratio = VALUE_HEADS // KEY_HEADS
    blocks = TOKENS // BLOCK
    margin = KERNEL - 1

    def regroup(source):
        return source.reshape((blocks, BLOCK) + source.shape[1:])
    inputs = (regroup(query_raw), regroup(key_raw), regroup(value_raw), regroup(gate_branch), regroup(gate_code), regroup(beta_code))
    start_state = jnp.zeros((VALUE_HEADS, HEAD_DIM, HEAD_DIM), jnp.float32)
    start_rims = (jnp.zeros((margin, query_raw.shape[1]), query_raw.dtype), jnp.zeros((margin, key_raw.shape[1]), key_raw.dtype), jnp.zeros((margin, value_raw.shape[1]), value_raw.dtype))

    def advance(loop_carry, pieces):
        carried, rim_rows = loop_carry
        query_piece, key_piece, value_piece, branch_piece, code_piece, beta_piece = pieces
        query_conv = causal_conv(rim_rows[0], query_piece, conv_query)
        key_conv = causal_conv(rim_rows[1], key_piece, conv_key)
        value_conv = causal_conv(rim_rows[2], value_piece, conv_value)
        queries = unit_rows(query_conv.reshape(BLOCK, KEY_HEADS, HEAD_DIM)) * HEAD_DIM ** (-0.5)
        key_rows = unit_rows(key_conv.reshape(BLOCK, KEY_HEADS, HEAD_DIM))
        queries = jnp.repeat(queries, group_ratio, axis=1).transpose(1, 0, 2)
        key_rows = jnp.repeat(key_rows, group_ratio, axis=1).transpose(1, 0, 2)
        value_rows = value_conv.reshape(BLOCK, VALUE_HEADS, HEAD_DIM).transpose(1, 0, 2)
        log_gate = jnp.log1p(-1e-06 * code_piece.astype(jnp.float32)).T
        strength = (beta_piece.astype(jnp.float32) / 1000.0).T
        gammas, mixing, wy_keys, wy_values, key_tails, block_decay = prepare(queries, key_rows, value_rows, log_gate, strength)
        fresh = wy_values - jnp.einsum('hid,hde->hie', wy_keys, carried, precision=EXACT)
        emitted = gammas[..., None] * jnp.einsum('hid,hde->hie', queries, carried, precision=EXACT)
        emitted = emitted + jnp.einsum('hij,hje->hie', mixing, fresh, precision=EXACT)
        carried = block_decay[:, None, None] * carried + jnp.einsum('hid,hie->hde', key_tails, fresh, precision=EXACT)
        normed = gated_norm(emitted.transpose(1, 0, 2), branch_piece, norm_gain)
        mixed_rows = jnp.dot(normed, out_weight, preferred_element_type=jnp.float32).astype(jnp.bfloat16)
        new_rims = (query_piece[BLOCK - margin:], key_piece[BLOCK - margin:], value_piece[BLOCK - margin:])
        return ((carried, new_rims), mixed_rows)
    _, outputs = lax.scan(advance, (start_state, start_rims), inputs)
    return outputs.reshape(TOKENS, D)
```

```python
import functools
import jax
import jax.numpy as jnp
from jax import lax
from jax.experimental import pallas as pl
from jax.experimental.pallas import tpu as pltpu
from jax.sharding import PartitionSpec as P

HEAD_DIM = 128
KERNEL = 4
BLOCK = 64
RIM = 16
F32 = jnp.float32
BF16 = jnp.bfloat16
EXACT = lax.Precision.HIGHEST
NT = (((1,), (1,)), ((), ()))


def passed_along(block, axis, distance):
    devices = range(lax.axis_size(axis))
    route = [(i - distance, i) for i in devices if i - distance in devices]
    return lax.ppermute(block, axis, route)


def split(x):
    hi = x.astype(BF16)
    return hi, (x - hi.astype(F32)).astype(BF16)


def dot(a, b):
    return jnp.dot(a, b, preferred_element_type=F32)


def dot_narrow(a, b):
    ah, al = split(a)
    bh, bl = split(b)
    return dot(jnp.concatenate([ah, ah, al], 1), jnp.concatenate([bh, bl, bh], 0))


def dot_wide(a, b):
    ah, al = split(a)
    bh, bl = split(b)
    return dot(jnp.concatenate([ah, al], 1), jnp.concatenate([bh, bh], 0)) + dot(ah, bl)


def dot_wide_nt(a, b):
    ah, al = split(a)
    bh, bl = split(b)
    both = lax.dot_general(
        jnp.concatenate([ah, al], 1),
        jnp.concatenate([bh, bh], 1),
        NT,
        preferred_element_type=F32,
    )
    return both + lax.dot_general(ah, bl, NT, preferred_element_type=F32)


def silu(x):
    return x / (1.0 + jnp.exp(-x))


def log_gates(code):
    x = code.astype(F32) * 1e-06
    return -x * (1.0 + x * (0.5 + x * (1.0 / 3.0 + x * 0.25)))


def local_kernel(
    q_ref, k_ref, v_ref, rim_ref, gate_ref, gate_t_ref, beta_ref, wq_ref, wk_ref, wv_ref,
    eb_ref, state_ref, tail_ref,
):
    rows, key_width = q_ref.shape
    value_width = v_ref.shape[1]
    key_heads = key_width // HEAD_DIM
    heads = value_width // HEAD_DIM
    ratio = heads // key_heads
    margin = KERNEL - 1
    row_ids = lax.broadcasted_iota(jnp.int32, (BLOCK, BLOCK), 0)
    col_ids = lax.broadcasted_iota(jnp.int32, (BLOCK, BLOCK), 1)
    causal = row_ids >= col_ids
    strict = row_ids > col_ids
    eye = (row_ids == col_ids).astype(F32)
    tri = causal.astype(F32)
    tri_t = (row_ids <= col_ids).astype(F32)
    eye_state = (
        lax.broadcasted_iota(jnp.int32, (HEAD_DIM, 2 * HEAD_DIM), 0)
        == lax.broadcasted_iota(jnp.int32, (HEAD_DIM, 2 * HEAD_DIM), 1)
    ).astype(F32)
    for h in range(heads):
        state_ref[h] = eye_state
    tail_ref[...] = rim_ref[...]

    def conv(ref, tap_ref, at, lo, width):
        now = ref[pl.ds(at, BLOCK), lo[0] : lo[0] + width]
        before = tail_ref[:, lo[1] : lo[1] + width]
        tail_ref[:, lo[1] : lo[1] + width] = now[BLOCK - RIM :]
        full = jnp.concatenate([before, now], 0).astype(F32)
        total = None
        for j in range(KERNEL):
            start = RIM - margin + j
            term = tap_ref[j : j + 1, lo[0] : lo[0] + width].astype(F32) * full[start : start + BLOCK]
            total = term if total is None else total + term
        return silu(total)

    def unit(x):
        return x * lax.rsqrt(jnp.sum(x * x, -1, keepdims=True) + 1e-06)

    def step(n, _):
        at = pl.multiple_of(n * BLOCK, BLOCK)
        cum = jnp.dot(tri, log_gates(gate_ref[pl.ds(at, BLOCK), :]), precision=EXACT, preferred_element_type=F32)
        cum_t = jnp.dot(log_gates(gate_t_ref[n]), tri_t, precision=EXACT, preferred_element_type=F32)
        strength = beta_ref[pl.ds(at, BLOCK), :].astype(F32) / 1000.0
        gamma = jnp.exp(cum)
        gamma_end = gamma[BLOCK - 1 :, :]
        inv_t = jnp.exp(-cum_t)
        bg = strength * gamma
        qs, ks, vs, kts, kks, qks = [], [], [], [], [], []
        for p in range(key_heads):
            lo = p * HEAD_DIM
            q = unit(conv(q_ref, wq_ref, at, (lo, lo), HEAD_DIM)) * HEAD_DIM ** (-0.5)
            k = unit(conv(k_ref, wk_ref, at, (lo, key_width + lo), HEAD_DIM))
            qs.append(q)
            ks.append(k)
            kts.append(k.T)
            both = dot_wide_nt(jnp.concatenate([k, q], 0), k)
            kks.append(both[:BLOCK])
            qks.append(both[BLOCK:])
        for h in range(heads):
            lo = h * HEAD_DIM
            vs.append(conv(v_ref, wv_ref, at, (lo, 2 * key_width + lo), HEAD_DIM))
        mixes, results, powers = [], [], []
        for h in range(heads):
            p = h // ratio
            row = inv_t[h : h + 1, :]
            mixes.append(jnp.where(causal, qks[p] * (gamma[:, h : h + 1] * row), 0.0))
            part = jnp.where(strict, kks[p] * (bg[:, h : h + 1] * row), 0.0)
            results.append(eye - part)
            powers.append(part)
        powers = [dot_narrow(a, a) for a in powers]
        covered = 4
        while covered < BLOCK:
            both = [dot_narrow(jnp.concatenate([r, a], 0), a) for r, a in zip(results, powers)]
            results = [r + b[:BLOCK] for r, b in zip(results, both)]
            powers = [b[BLOCK:] for b in both]
            covered = covered * 2
        results = [r + dot_narrow(r, a) for r, a in zip(results, powers)]
        wys = []
        for h in range(heads):
            p = h // ratio
            right = jnp.concatenate([bg[:, h : h + 1] * ks[p], strength[:, h : h + 1] * vs[h]], 1)
            wys.append(dot_narrow(results[h], right))
        seen = []
        for h in range(heads):
            left = jnp.concatenate([wys[h][:, :HEAD_DIM], gamma[:, h : h + 1] * qs[h // ratio]], 0)
            seen.append(dot_wide(left, state_ref[h]))
        zeros = jnp.zeros((BLOCK, HEAD_DIM), F32)
        for h in range(heads):
            fresh = jnp.concatenate([zeros, wys[h][:, HEAD_DIM:]], 1) - seen[h][:BLOCK]
            end = gamma_end[:, h : h + 1]
            left = jnp.concatenate([kts[h // ratio] * (end * inv_t[h : h + 1, :]), mixes[h]], 0)
            moved = dot_narrow(left, fresh)
            state_ref[h] = end * state_ref[h] + moved[:HEAD_DIM]
            eb_ref[pl.ds(at, BLOCK), 2 * h * HEAD_DIM : 2 * (h + 1) * HEAD_DIM] = (
                seen[h][BLOCK:] + moved[HEAD_DIM:]
            )
        return 0

    lax.fori_loop(0, rows // BLOCK, step, 0)


def emit_kernel(eb_ref, branch_ref, state_ref, gain_ref, weight_ref, out_ref, y_ref):
    heads = state_ref.shape[0]
    gain = gain_ref[...]
    for h in range(heads):
        lo = 2 * h * HEAD_DIM
        o = eb_ref[:, lo + HEAD_DIM : lo + 2 * HEAD_DIM] + dot_wide(
            eb_ref[:, lo : lo + HEAD_DIM], state_ref[h]
        )
        scaled = o * lax.rsqrt(jnp.mean(o * o, -1, keepdims=True) + 1e-06) * gain
        gating = silu(branch_ref[:, h * HEAD_DIM : (h + 1) * HEAD_DIM].astype(F32))
        y_ref[:, h * HEAD_DIM : (h + 1) * HEAD_DIM] = (scaled * gating).astype(BF16)
    out_ref[...] = dot(y_ref[...], weight_ref[...])


def shards(
    query_raw, key_raw, value_raw, gate_branch, gate_code, beta_code,
    conv_query, conv_key, conv_value, norm_gain, out_weight,
):
    rows, key_width = query_raw.shape
    value_width = value_raw.shape[1]
    heads = value_width // HEAD_DIM
    blocks = rows // BLOCK
    model = out_weight.shape[1]
    rims = passed_along(
        jnp.concatenate([x[rows - RIM :] for x in (query_raw, key_raw, value_raw)], 1), "ctx", 1
    )
    gate_t = gate_code.reshape(blocks, BLOCK, heads).transpose(0, 2, 1)
    vmem = pl.BlockSpec(memory_space=pltpu.VMEM)
    eb, state = pl.pallas_call(
        local_kernel,
        out_shape=(
            jax.ShapeDtypeStruct((rows, 2 * value_width), F32),
            jax.ShapeDtypeStruct((heads, HEAD_DIM, 2 * HEAD_DIM), F32),
        ),
        in_specs=[vmem] * 10,
        out_specs=(vmem, vmem),
        scratch_shapes=[pltpu.VMEM((RIM, 2 * key_width + value_width), BF16)],
        compiler_params=pltpu.CompilerParams(vmem_limit_bytes=56 * 1024 * 1024),
        name="local_scan",
    )(query_raw, key_raw, value_raw, rims, gate_code, gate_t, beta_code, conv_query, conv_key, conv_value)
    dev_map, dev_sum = state[:, :, :HEAD_DIM], state[:, :, HEAD_DIM:]
    position = lax.axis_index("ctx")

    def relay_hop(hop_index, received):
        outgoing = jnp.matmul(dev_map, received, precision=lax.Precision.HIGH) + dev_sum
        arrived = passed_along(outgoing, "ctx", 1)
        return jnp.where(position == hop_index, arrived, received)

    incoming = lax.fori_loop(1, lax.axis_size("ctx"), relay_hop, jnp.zeros_like(dev_sum))
    tile = min(rows, 128)
    partial = pl.pallas_call(
        emit_kernel,
        grid=(rows // tile,),
        out_shape=jax.ShapeDtypeStruct((rows, model), F32),
        in_specs=[
            pl.BlockSpec((tile, 2 * value_width), lambda i: (i, 0)),
            pl.BlockSpec((tile, value_width), lambda i: (i, 0)),
            pl.BlockSpec((heads, HEAD_DIM, HEAD_DIM), lambda i: (0, 0, 0)),
            pl.BlockSpec((1, HEAD_DIM), lambda i: (0, 0)),
            pl.BlockSpec((value_width, model), lambda i: (0, 0)),
        ],
        out_specs=pl.BlockSpec((tile, model), lambda i: (i, 0)),
        scratch_shapes=[pltpu.VMEM((tile, value_width), BF16)],
        compiler_params=pltpu.CompilerParams(vmem_limit_bytes=48 * 1024 * 1024),
        name="emit",
    )(eb, gate_branch, incoming, norm_gain.reshape(1, HEAD_DIM), out_weight)
    return lax.psum_scatter(partial, "head", scatter_dimension=0, tiled=True).astype(BF16)


def solution(mesh):
    return jax.shard_map(
        shards,
        mesh=mesh,
        in_specs=(P("ctx", "head"),) * 6 + (P(None, "head"),) * 3 + (P(), P("head", None)),
        out_specs=P(("ctx", "head"), None),
        check_vma=False,
    )
```

```python
import functools
import jax
import jax.numpy as jnp
from jax import lax
from jax.experimental import pallas as pl
from jax.experimental.pallas import tpu as pltpu
from jax.sharding import PartitionSpec as P

HEAD_DIM = 128
KERNEL = 4
BLOCK = 64
RIM = 16
F32 = jnp.float32
BF16 = jnp.bfloat16
EXACT = lax.Precision.HIGHEST
NT = (((1,), (1,)), ((), ()))


def passed_along(block, axis, distance):
    devices = range(lax.axis_size(axis))
    route = [(i - distance, i) for i in devices if i - distance in devices]
    return lax.ppermute(block, axis, route)


def split(x):
    hi = x.astype(BF16)
    return hi, (x - hi.astype(F32)).astype(BF16)


def dot(a, b):
    return jnp.dot(a, b, preferred_element_type=F32)


def dot_narrow(a, b):
    ah, al = split(a)
    bh, bl = split(b)
    return dot(jnp.concatenate([ah, ah, al], 1), jnp.concatenate([bh, bl, bh], 0))


def dot_wide(a, b):
    ah, al = split(a)
    bh, bl = split(b)
    return dot(jnp.concatenate([ah, al], 1), jnp.concatenate([bh, bh], 0)) + dot(ah, bl)


def dot_wide_nt(a, b):
    ah, al = split(a)
    bh, bl = split(b)
    both = lax.dot_general(
        jnp.concatenate([ah, al], 1),
        jnp.concatenate([bh, bh], 1),
        NT,
        preferred_element_type=F32,
    )
    return both + lax.dot_general(ah, bl, NT, preferred_element_type=F32)


def silu(x):
    return x / (1.0 + jnp.exp(-x))


def log_gates(code):
    x = code.astype(F32) * 1e-06
    return -x * (1.0 + x * (0.5 + x * (1.0 / 3.0 + x * 0.25)))


def local_kernel(
    q_ref, k_ref, v_ref, rim_ref, gate_ref, gate_t_ref, beta_ref, wq_ref, wk_ref, wv_ref,
    eb_ref, state_ref, tail_ref,
):
    rows, key_width = q_ref.shape
    value_width = v_ref.shape[1]
    key_heads = key_width // HEAD_DIM
    heads = value_width // HEAD_DIM
    ratio = heads // key_heads
    margin = KERNEL - 1
    row_ids = lax.broadcasted_iota(jnp.int32, (BLOCK, BLOCK), 0)
    col_ids = lax.broadcasted_iota(jnp.int32, (BLOCK, BLOCK), 1)
    causal = row_ids >= col_ids
    strict = row_ids > col_ids
    eye = (row_ids == col_ids).astype(F32)
    tri = causal.astype(F32)
    tri_t = (row_ids <= col_ids).astype(F32)
    eye_state = (
        lax.broadcasted_iota(jnp.int32, (HEAD_DIM, 2 * HEAD_DIM), 0)
        == lax.broadcasted_iota(jnp.int32, (HEAD_DIM, 2 * HEAD_DIM), 1)
    ).astype(F32)
    for h in range(heads):
        state_ref[h] = eye_state
    tail_ref[...] = rim_ref[...]

    def conv(ref, tap_ref, at, lo, width):
        now = ref[pl.ds(at, BLOCK), lo[0] : lo[0] + width]
        before = tail_ref[:, lo[1] : lo[1] + width]
        tail_ref[:, lo[1] : lo[1] + width] = now[BLOCK - RIM :]
        full = jnp.concatenate([before, now], 0).astype(F32)
        total = None
        for j in range(KERNEL):
            start = RIM - margin + j
            term = tap_ref[j : j + 1, lo[0] : lo[0] + width].astype(F32) * full[start : start + BLOCK]
            total = term if total is None else total + term
        return silu(total)

    def unit(x):
        return x * lax.rsqrt(jnp.sum(x * x, -1, keepdims=True) + 1e-06)

    def step(n, _):
        at = pl.multiple_of(n * BLOCK, BLOCK)
        cum = jnp.dot(tri, log_gates(gate_ref[pl.ds(at, BLOCK), :]), precision=EXACT, preferred_element_type=F32)
        cum_t = jnp.dot(log_gates(gate_t_ref[n]), tri_t, precision=EXACT, preferred_element_type=F32)
        strength = beta_ref[pl.ds(at, BLOCK), :].astype(F32) / 1000.0
        gamma = jnp.exp(cum)
        gamma_end = gamma[BLOCK - 1 :, :]
        inv_t = jnp.exp(-cum_t)
        bg = strength * gamma
        qs, ks, vs, kts, kks, qks = [], [], [], [], [], []
        for p in range(key_heads):
            lo = p * HEAD_DIM
            q = unit(conv(q_ref, wq_ref, at, (lo, lo), HEAD_DIM)) * HEAD_DIM ** (-0.5)
            k = unit(conv(k_ref, wk_ref, at, (lo, key_width + lo), HEAD_DIM))
            qs.append(q)
            ks.append(k)
            kts.append(k.T)
            both = dot_wide_nt(jnp.concatenate([k, q], 0), k)
            kks.append(both[:BLOCK])
            qks.append(both[BLOCK:])
        for h in range(heads):
            lo = h * HEAD_DIM
            vs.append(conv(v_ref, wv_ref, at, (lo, 2 * key_width + lo), HEAD_DIM))
        mixes, results, powers = [], [], []
        for h in range(heads):
            p = h // ratio
            row = inv_t[h : h + 1, :]
            mixes.append(jnp.where(causal, qks[p] * (gamma[:, h : h + 1] * row), 0.0))
            part = jnp.where(strict, kks[p] * (bg[:, h : h + 1] * row), 0.0)
            results.append(eye - part)
            powers.append(part)
        powers = [dot_narrow(a, a) for a in powers]
        covered = 4
        while covered < BLOCK:
            both = [dot_narrow(jnp.concatenate([r, a], 0), a) for r, a in zip(results, powers)]
            results = [r + b[:BLOCK] for r, b in zip(results, both)]
            powers = [b[BLOCK:] for b in both]
            covered = covered * 2
        results = [r + dot_narrow(r, a) for r, a in zip(results, powers)]
        wys = []
        for h in range(heads):
            p = h // ratio
            right = jnp.concatenate([bg[:, h : h + 1] * ks[p], strength[:, h : h + 1] * vs[h]], 1)
            wys.append(dot_narrow(results[h], right))
        seen = []
        for h in range(heads):
            left = jnp.concatenate([wys[h][:, :HEAD_DIM], gamma[:, h : h + 1] * qs[h // ratio]], 0)
            seen.append(dot_wide(left, state_ref[h]))
        zeros = jnp.zeros((BLOCK, HEAD_DIM), F32)
        for h in range(heads):
            fresh = jnp.concatenate([zeros, wys[h][:, HEAD_DIM:]], 1) - seen[h][:BLOCK]
            end = gamma_end[:, h : h + 1]
            left = jnp.concatenate([kts[h // ratio] * (end * inv_t[h : h + 1, :]), mixes[h]], 0)
            moved = dot_narrow(left, fresh)
            state_ref[h] = end * state_ref[h] + moved[:HEAD_DIM]
            eb_ref[pl.ds(at, BLOCK), 2 * h * HEAD_DIM : 2 * (h + 1) * HEAD_DIM] = (
                seen[h][BLOCK:] + moved[HEAD_DIM:]
            )
        return 0

    lax.fori_loop(0, rows // BLOCK, step, 0)


MESH = pl.DeviceIdType.MESH
LEVELS = 32760.0


def relay_kernel(count, state_ref, in_ref, landed, outgoing, send_sem, recv_sem):
    heads = state_ref.shape[0]
    place = lax.axis_index("ctx")
    later = lax.rem(place + 1, count)
    earlier = lax.rem(place + count - 1, count)
    has_earlier = place > 0
    has_later = place < count - 1
    barrier = pltpu.get_barrier_semaphore()

    @pl.when(has_earlier)
    def _():
        pl.semaphore_signal(barrier, inc=1, device_id={"ctx": earlier}, device_id_type=MESH)

    @pl.when(has_later)
    def _():
        pl.semaphore_signal(barrier, inc=1, device_id={"ctx": later}, device_id_type=MESH)

    inner = jnp.logical_and(has_earlier, has_later)

    @pl.when(inner)
    def _():
        pl.semaphore_wait(barrier, 2)

    @pl.when(jnp.logical_not(inner))
    def _():
        pl.semaphore_wait(barrier, 1)

    @pl.when(place == 0)
    def _():
        landed[...] = jnp.zeros_like(landed)

    def hop(h):
        return pltpu.make_async_remote_copy(
            src_ref=outgoing.at[h],
            dst_ref=landed.at[h],
            send_sem=send_sem.at[h],
            recv_sem=recv_sem.at[h],
            device_id={"ctx": later},
            device_id_type=MESH,
        )

    for h in range(heads):

        @pl.when(has_earlier)
        def _():
            hop(h).wait_recv()

        @pl.when(has_later)
        def _():
            outgoing[h] = dot_wide(state_ref[h, :, :HEAD_DIM], landed[h]) + state_ref[h, :, HEAD_DIM:]
            hop(h).start()

    in_ref[...] = landed[...]
    for h in range(heads):

        @pl.when(has_later)
        def _():
            hop(h).wait_send()


def emit_kernel(
    count, eb_ref, branch_ref, state_ref, gain_ref, weight_ref, out_ref,
    y_ref, part_out, part_in, code_out, code_in, scale_out, scale_in,
    part_send, part_recv, code_send, code_recv, scale_send, scale_recv,
):
    heads = state_ref.shape[0]
    chunk, model = code_out.shape[2:]
    quarter = out_ref.shape[0]
    chunks = quarter // chunk
    gain = gain_ref[...]
    me = lax.axis_index("head")
    mate = me + 1 - 2 * lax.rem(me, 2)

    barrier = pltpu.get_barrier_semaphore()
    for other in [mate] + [lax.rem(me + 2 * d, count) for d in range(1, count // 2)]:
        pl.semaphore_signal(barrier, inc=1, device_id={"head": other}, device_id_type=MESH)
    pl.semaphore_wait(barrier, count // 2)

    def partial(owner, c):
        at = pl.multiple_of(owner * quarter + c * chunk, chunk)
        for h in range(heads):
            lo = 2 * h * HEAD_DIM
            o = eb_ref[pl.ds(at, chunk), lo + HEAD_DIM : lo + 2 * HEAD_DIM] + dot_wide(
                eb_ref[pl.ds(at, chunk), lo : lo + HEAD_DIM], state_ref[h]
            )
            scaled = o * lax.rsqrt(jnp.mean(o * o, -1, keepdims=True) + 1e-06) * gain
            gating = silu(branch_ref[pl.ds(at, chunk), h * HEAD_DIM : (h + 1) * HEAD_DIM].astype(F32))
            y_ref[:, h * HEAD_DIM : (h + 1) * HEAD_DIM] = (scaled * gating).astype(BF16)
        return dot(y_ref[...], weight_ref[...])

    def remote(source, target, sent, received, index, device):
        return pltpu.make_async_remote_copy(
            src_ref=source.at[index],
            dst_ref=target.at[index],
            send_sem=sent.at[index],
            recv_sem=received.at[index],
            device_id={"head": device},
            device_id_type=MESH,
        )

    def part(d, c):
        return remote(part_out, part_in, part_send, part_recv, (d, c), mate)

    def coded(d, c):
        peer = lax.rem(me + 2 * d, count)
        return (
            remote(code_out, code_in, code_send, code_recv, (d - 1, c), peer),
            remote(scale_out, scale_in, scale_send, scale_recv, (d - 1, c), peer),
        )

    def shared(d, c):
        part_out[d, c] = partial(lax.rem(mate + 2 * d, count), c)
        part(d, c).start()
        mine = partial(lax.rem(me + 2 * d, count), c)
        part(d, c).wait_recv()
        return mine + part_in[d, c]

    for d in range(1, count // 2):

        def forward(c, _):
            total = shared(d, c)
            groups = jnp.abs(total).reshape(chunk // 8, 8, model)
            top = jnp.max(jnp.max(groups, axis=0), axis=-1, keepdims=True)
            top = jnp.maximum(top, 1e-30)
            scale_out[d - 1, c] = jnp.broadcast_to(top * (1.0 / LEVELS), (8, 128))
            rate = jnp.broadcast_to((LEVELS / top)[None], (chunk // 8, 8, 1)).reshape(chunk, 1)
            code_out[d - 1, c] = jnp.floor(total * rate + 0.5).astype(jnp.int32).astype(jnp.int16)
            for copy in coded(d, c):
                copy.start()
            return 0

        lax.fori_loop(0, chunks, forward, 0)

    def own(c, _):
        at = pl.multiple_of(c * chunk, chunk)
        total = shared(0, c)
        for d in range(1, count // 2):
            for copy in coded(d, c):
                copy.wait_recv()
            unit = scale_in[d - 1, c][:, :1]
            unit = jnp.broadcast_to(unit[None], (chunk // 8, 8, 1)).reshape(chunk, 1)
            total = total + code_in[d - 1, c].astype(jnp.int32).astype(F32) * unit
        out_ref[pl.ds(at, chunk), :] = total.astype(BF16)
        return 0

    lax.fori_loop(0, chunks, own, 0)

    def drain(c, _):
        for d in range(count // 2):
            part(d, c).wait_send()
        for d in range(1, count // 2):
            for copy in coded(d, c):
                copy.wait_send()
        return 0

    lax.fori_loop(0, chunks, drain, 0)


def shards(
    query_raw, key_raw, value_raw, gate_branch, gate_code, beta_code,
    conv_query, conv_key, conv_value, norm_gain, out_weight,
):
    rows, key_width = query_raw.shape
    value_width = value_raw.shape[1]
    heads = value_width // HEAD_DIM
    blocks = rows // BLOCK
    model = out_weight.shape[1]
    rims = passed_along(
        jnp.concatenate([x[rows - RIM :] for x in (query_raw, key_raw, value_raw)], 1), "ctx", 1
    )
    gate_t = gate_code.reshape(blocks, BLOCK, heads).transpose(0, 2, 1)
    vmem = pl.BlockSpec(memory_space=pltpu.VMEM)
    eb, state = pl.pallas_call(
        local_kernel,
        out_shape=(
            jax.ShapeDtypeStruct((rows, 2 * value_width), F32),
            jax.ShapeDtypeStruct((heads, HEAD_DIM, 2 * HEAD_DIM), F32),
        ),
        in_specs=[vmem] * 10,
        out_specs=(vmem, vmem),
        scratch_shapes=[pltpu.VMEM((RIM, 2 * key_width + value_width), BF16)],
        compiler_params=pltpu.CompilerParams(vmem_limit_bytes=56 * 1024 * 1024),
        name="local_scan",
    )(query_raw, key_raw, value_raw, rims, gate_code, gate_t, beta_code, conv_query, conv_key, conv_value)
    places = lax.axis_size("ctx")
    incoming = pl.pallas_call(
        functools.partial(relay_kernel, places),
        out_shape=jax.ShapeDtypeStruct((heads, HEAD_DIM, HEAD_DIM), F32),
        in_specs=[vmem],
        out_specs=vmem,
        scratch_shapes=[
            pltpu.VMEM((heads, HEAD_DIM, HEAD_DIM), F32),
            pltpu.VMEM((heads, HEAD_DIM, HEAD_DIM), F32),
            pltpu.SemaphoreType.DMA((heads,)),
            pltpu.SemaphoreType.DMA((heads,)),
        ],
        compiler_params=pltpu.CompilerParams(
            collective_id=0, has_side_effects=True, vmem_limit_bytes=32 * 1024 * 1024
        ),
        name="relay",
    )(state)
    count = lax.axis_size("head")
    quarter = rows // count
    chunk = min(quarter, 128)
    chunks = quarter // chunk
    near = (count // 2, chunks)
    far = (max(count // 2 - 1, 1), chunks)
    return pl.pallas_call(
        functools.partial(emit_kernel, count),
        out_shape=jax.ShapeDtypeStruct((quarter, model), BF16),
        in_specs=[vmem] * 5,
        out_specs=vmem,
        scratch_shapes=[
            pltpu.VMEM((chunk, value_width), BF16),
            pltpu.VMEM(near + (chunk, model), F32),
            pltpu.VMEM(near + (chunk, model), F32),
            pltpu.VMEM(far + (chunk, model), jnp.int16),
            pltpu.VMEM(far + (chunk, model), jnp.int16),
            pltpu.VMEM(far + (8, 128), F32),
            pltpu.VMEM(far + (8, 128), F32),
        ]
        + [pltpu.SemaphoreType.DMA(near)] * 2
        + [pltpu.SemaphoreType.DMA(far)] * 4,
        compiler_params=pltpu.CompilerParams(
            collective_id=1, has_side_effects=True, vmem_limit_bytes=56 * 1024 * 1024
        ),
        name="emit_scatter",
    )(eb, gate_branch, incoming, norm_gain.reshape(1, HEAD_DIM), out_weight)


def solution(mesh):
    return jax.shard_map(
        shards,
        mesh=mesh,
        in_specs=(P("ctx", "head"),) * 6 + (P(None, "head"),) * 3 + (P(), P("head", None)),
        out_specs=P(("ctx", "head"), None),
        check_vma=False,
    )
```

```python
import functools
import jax
import jax.numpy as jnp
from jax import lax
from jax.experimental import pallas as pl
from jax.experimental.pallas import tpu as pltpu
from jax.sharding import PartitionSpec as P

HEAD_DIM = 128
KERNEL = 4
BLOCK = 64
RIM = 16
F32 = jnp.float32
BF16 = jnp.bfloat16
EXACT = lax.Precision.HIGHEST
NT = (((1,), (1,)), ((), ()))


def passed_along(block, axis, distance):
    devices = range(lax.axis_size(axis))
    route = [(i - distance, i) for i in devices if i - distance in devices]
    return lax.ppermute(block, axis, route)


def split(x):
    hi = x.astype(BF16)
    return hi, (x - hi.astype(F32)).astype(BF16)


def dot(a, b):
    return jnp.dot(a, b, preferred_element_type=F32)


def dot_narrow(a, b):
    ah, al = split(a)
    bh, bl = split(b)
    return dot(jnp.concatenate([ah, ah, al], 1), jnp.concatenate([bh, bl, bh], 0))


def dot_wide(a, b):
    ah, al = split(a)
    bh, bl = split(b)
    return dot(jnp.concatenate([ah, al], 1), jnp.concatenate([bh, bh], 0)) + dot(ah, bl)


def dot_wide_nt(a, b):
    ah, al = split(a)
    bh, bl = split(b)
    both = lax.dot_general(
        jnp.concatenate([ah, al], 1),
        jnp.concatenate([bh, bh], 1),
        NT,
        preferred_element_type=F32,
    )
    return both + lax.dot_general(ah, bl, NT, preferred_element_type=F32)


def silu(x):
    return x / (1.0 + jnp.exp(-x))


def log_gates(code):
    x = code.astype(F32) * 1e-06
    return -x * (1.0 + x * (0.5 + x * (1.0 / 3.0 + x * 0.25)))


def local_kernel(
    q_ref, k_ref, v_ref, rim_ref, gate_t_ref, beta_t_ref, wq_ref, wk_ref, wv_ref,
    eb_ref, state_ref, tail_ref,
):
    rows, key_width = q_ref.shape
    value_width = v_ref.shape[1]
    key_heads = key_width // HEAD_DIM
    heads = value_width // HEAD_DIM
    ratio = heads // key_heads
    margin = KERNEL - 1
    row_ids = lax.broadcasted_iota(jnp.int32, (BLOCK, BLOCK), 0)
    col_ids = lax.broadcasted_iota(jnp.int32, (BLOCK, BLOCK), 1)
    causal = row_ids >= col_ids
    strict = row_ids > col_ids
    eye = (row_ids == col_ids).astype(F32)
    tri_t = (row_ids <= col_ids).astype(F32)
    eye_state = (
        lax.broadcasted_iota(jnp.int32, (HEAD_DIM, 2 * HEAD_DIM), 0)
        == lax.broadcasted_iota(jnp.int32, (HEAD_DIM, 2 * HEAD_DIM), 1)
    ).astype(F32)
    for h in range(heads):
        state_ref[h] = eye_state
    tail_ref[...] = rim_ref[...]

    def conv(ref, tap_ref, at, lo, width):
        now = ref[pl.ds(at, BLOCK), lo[0] : lo[0] + width]
        before = tail_ref[:, lo[1] : lo[1] + width]
        tail_ref[:, lo[1] : lo[1] + width] = now[BLOCK - RIM :]
        full = jnp.concatenate([before, now], 0).astype(F32)
        total = None
        for j in range(KERNEL):
            start = RIM - margin + j
            term = tap_ref[j : j + 1, lo[0] : lo[0] + width].astype(F32) * full[start : start + BLOCK]
            total = term if total is None else total + term
        return silu(total)

    def unit(x):
        return x * lax.rsqrt(jnp.sum(x * x, -1, keepdims=True) + 1e-06)

    def step(n, _):
        at = pl.multiple_of(n * BLOCK, BLOCK)
        cum_t = jnp.dot(log_gates(gate_t_ref[n]), tri_t, precision=EXACT, preferred_element_type=F32)
        cum = cum_t.T
        strength = (beta_t_ref[n].astype(F32) / 1000.0).T
        gamma = jnp.exp(cum)
        gamma_end = gamma[BLOCK - 1 :, :]
        inv_t = jnp.exp(-cum_t)
        bg = strength * gamma
        qs, ks, vs, kts, kks, qks = [], [], [], [], [], []
        for p in range(key_heads):
            lo = p * HEAD_DIM
            q = unit(conv(q_ref, wq_ref, at, (lo, lo), HEAD_DIM)) * HEAD_DIM ** (-0.5)
            k = unit(conv(k_ref, wk_ref, at, (lo, key_width + lo), HEAD_DIM))
            qs.append(q)
            ks.append(k)
            kts.append(k.T)
            both = dot_wide_nt(jnp.concatenate([k, q], 0), k)
            kks.append(both[:BLOCK])
            qks.append(both[BLOCK:])
        for h in range(heads):
            lo = h * HEAD_DIM
            vs.append(conv(v_ref, wv_ref, at, (lo, 2 * key_width + lo), HEAD_DIM))
        mixes, results, powers = [], [], []
        for h in range(heads):
            p = h // ratio
            row = inv_t[h : h + 1, :]
            mixes.append(jnp.where(causal, qks[p] * (gamma[:, h : h + 1] * row), 0.0))
            part = jnp.where(strict, kks[p] * (bg[:, h : h + 1] * row), 0.0)
            results.append(eye - part)
            powers.append(part)
        powers = [dot_narrow(a, a) for a in powers]
        covered = 4
        while covered < BLOCK:
            both = [dot_narrow(jnp.concatenate([r, a], 0), a) for r, a in zip(results, powers)]
            results = [r + b[:BLOCK] for r, b in zip(results, both)]
            powers = [b[BLOCK:] for b in both]
            covered = covered * 2
        results = [r + dot_narrow(r, a) for r, a in zip(results, powers)]
        wys = []
        for h in range(heads):
            p = h // ratio
            right = jnp.concatenate([bg[:, h : h + 1] * ks[p], strength[:, h : h + 1] * vs[h]], 1)
            wys.append(dot_narrow(results[h], right))
        seen = []
        for h in range(heads):
            left = jnp.concatenate([wys[h][:, :HEAD_DIM], gamma[:, h : h + 1] * qs[h // ratio]], 0)
            seen.append(dot_wide(left, state_ref[h]))
        zeros = jnp.zeros((BLOCK, HEAD_DIM), F32)
        for h in range(heads):
            fresh = jnp.concatenate([zeros, wys[h][:, HEAD_DIM:]], 1) - seen[h][:BLOCK]
            end = gamma_end[:, h : h + 1]
            left = jnp.concatenate([kts[h // ratio] * (end * inv_t[h : h + 1, :]), mixes[h]], 0)
            moved = dot_narrow(left, fresh)
            state_ref[h] = end * state_ref[h] + moved[:HEAD_DIM]
            eb_ref[pl.ds(at, BLOCK), 2 * h * HEAD_DIM : 2 * (h + 1) * HEAD_DIM] = (
                seen[h][BLOCK:] + moved[HEAD_DIM:]
            )
        return 0

    lax.fori_loop(0, rows // BLOCK, step, 0)


MESH = pl.DeviceIdType.MESH
LEVELS = 32760.0


def relay_kernel(count, state_ref, in_ref, landed, outgoing, send_sem, recv_sem):
    heads = state_ref.shape[0]
    place = lax.axis_index("ctx")
    later = lax.rem(place + 1, count)
    earlier = lax.rem(place + count - 1, count)
    has_earlier = place > 0
    has_later = place < count - 1
    barrier = pltpu.get_barrier_semaphore()

    @pl.when(has_earlier)
    def _():
        pl.semaphore_signal(barrier, inc=1, device_id={"ctx": earlier}, device_id_type=MESH)

    @pl.when(has_later)
    def _():
        pl.semaphore_signal(barrier, inc=1, device_id={"ctx": later}, device_id_type=MESH)

    inner = jnp.logical_and(has_earlier, has_later)

    @pl.when(inner)
    def _():
        pl.semaphore_wait(barrier, 2)

    @pl.when(jnp.logical_not(inner))
    def _():
        pl.semaphore_wait(barrier, 1)

    @pl.when(place == 0)
    def _():
        landed[...] = jnp.zeros_like(landed)

    def hop(h):
        return pltpu.make_async_remote_copy(
            src_ref=outgoing.at[h],
            dst_ref=landed.at[h],
            send_sem=send_sem.at[h],
            recv_sem=recv_sem.at[h],
            device_id={"ctx": later},
            device_id_type=MESH,
        )

    for h in range(heads):

        @pl.when(has_earlier)
        def _():
            hop(h).wait_recv()

        @pl.when(has_later)
        def _():
            outgoing[h] = dot_wide(state_ref[h, :, :HEAD_DIM], landed[h]) + state_ref[h, :, HEAD_DIM:]
            hop(h).start()

    in_ref[...] = landed[...]
    for h in range(heads):

        @pl.when(has_later)
        def _():
            hop(h).wait_send()


def emit_kernel(
    count, eb_ref, branch_ref, state_ref, gain_ref, weight_ref, out_ref,
    y_ref, part_out, part_in, code_out, code_in, scale_out, scale_in,
    part_send, part_recv, code_send, code_recv, scale_send, scale_recv,
):
    heads = state_ref.shape[0]
    chunk, model = code_out.shape[2:]
    quarter = out_ref.shape[0]
    chunks = quarter // chunk
    gain = gain_ref[...]
    me = lax.axis_index("head")
    mate = me + 1 - 2 * lax.rem(me, 2)

    barrier = pltpu.get_barrier_semaphore()
    for other in [mate] + [lax.rem(me + 2 * d, count) for d in range(1, count // 2)]:
        pl.semaphore_signal(barrier, inc=1, device_id={"head": other}, device_id_type=MESH)
    pl.semaphore_wait(barrier, count // 2)

    def partial(owner, c):
        at = pl.multiple_of(owner * quarter + c * chunk, chunk)
        for h in range(heads):
            lo = 2 * h * HEAD_DIM
            o = eb_ref[pl.ds(at, chunk), lo + HEAD_DIM : lo + 2 * HEAD_DIM] + dot_wide(
                eb_ref[pl.ds(at, chunk), lo : lo + HEAD_DIM], state_ref[h]
            )
            scaled = o * lax.rsqrt(jnp.mean(o * o, -1, keepdims=True) + 1e-06) * gain
            gating = silu(branch_ref[pl.ds(at, chunk), h * HEAD_DIM : (h + 1) * HEAD_DIM].astype(F32))
            y_ref[:, h * HEAD_DIM : (h + 1) * HEAD_DIM] = (scaled * gating).astype(BF16)
        return dot(y_ref[...], weight_ref[...])

    def remote(source, target, sent, received, index, device):
        return pltpu.make_async_remote_copy(
            src_ref=source.at[index],
            dst_ref=target.at[index],
            send_sem=sent.at[index],
            recv_sem=received.at[index],
            device_id={"head": device},
            device_id_type=MESH,
        )

    def part(d, c):
        return remote(part_out, part_in, part_send, part_recv, (d, c), mate)

    def coded(d, c):
        peer = lax.rem(me + 2 * d, count)
        return (
            remote(code_out, code_in, code_send, code_recv, (d - 1, c), peer),
            remote(scale_out, scale_in, scale_send, scale_recv, (d - 1, c), peer),
        )

    def shared(d, c):
        part_out[d, c] = partial(lax.rem(mate + 2 * d, count), c)
        part(d, c).start()
        mine = partial(lax.rem(me + 2 * d, count), c)
        part(d, c).wait_recv()
        return mine + part_in[d, c]

    for d in range(1, count // 2):

        def forward(c, _):
            total = shared(d, c)
            groups = jnp.abs(total).reshape(chunk // 8, 8, model)
            top = jnp.max(jnp.max(groups, axis=0), axis=-1, keepdims=True)
            top = jnp.maximum(top, 1e-30)
            scale_out[d - 1, c] = jnp.broadcast_to(top * (1.0 / LEVELS), (8, 128))
            rate = jnp.broadcast_to((LEVELS / top)[None], (chunk // 8, 8, 1)).reshape(chunk, 1)
            code_out[d - 1, c] = jnp.floor(total * rate + 0.5).astype(jnp.int32).astype(jnp.int16)
            for copy in coded(d, c):
                copy.start()
            return 0

        lax.fori_loop(0, chunks, forward, 0)

    def own(c, _):
        at = pl.multiple_of(c * chunk, chunk)
        total = shared(0, c)
        for d in range(1, count // 2):
            for copy in coded(d, c):
                copy.wait_recv()
            unit = scale_in[d - 1, c][:, :1]
            unit = jnp.broadcast_to(unit[None], (chunk // 8, 8, 1)).reshape(chunk, 1)
            total = total + code_in[d - 1, c].astype(jnp.int32).astype(F32) * unit
        out_ref[pl.ds(at, chunk), :] = total.astype(BF16)
        return 0

    lax.fori_loop(0, chunks, own, 0)

    def drain(c, _):
        for d in range(count // 2):
            part(d, c).wait_send()
        for d in range(1, count // 2):
            for copy in coded(d, c):
                copy.wait_send()
        return 0

    lax.fori_loop(0, chunks, drain, 0)


def shards(
    query_raw, key_raw, value_raw, gate_branch, gate_code, beta_code,
    conv_query, conv_key, conv_value, norm_gain, out_weight,
):
    rows, key_width = query_raw.shape
    value_width = value_raw.shape[1]
    heads = value_width // HEAD_DIM
    blocks = rows // BLOCK
    model = out_weight.shape[1]
    rims = passed_along(
        jnp.concatenate([x[rows - RIM :] for x in (query_raw, key_raw, value_raw)], 1), "ctx", 1
    )
    gate_t, beta_t = (
        x.reshape(blocks, BLOCK, heads).transpose(0, 2, 1) for x in (gate_code, beta_code)
    )
    vmem = pl.BlockSpec(memory_space=pltpu.VMEM)
    eb, state = pl.pallas_call(
        local_kernel,
        out_shape=(
            jax.ShapeDtypeStruct((rows, 2 * value_width), F32),
            jax.ShapeDtypeStruct((heads, HEAD_DIM, 2 * HEAD_DIM), F32),
        ),
        in_specs=[vmem] * 9,
        out_specs=(vmem, vmem),
        scratch_shapes=[pltpu.VMEM((RIM, 2 * key_width + value_width), BF16)],
        compiler_params=pltpu.CompilerParams(vmem_limit_bytes=56 * 1024 * 1024),
        name="local_scan",
    )(query_raw, key_raw, value_raw, rims, gate_t, beta_t, conv_query, conv_key, conv_value)
    places = lax.axis_size("ctx")
    incoming = pl.pallas_call(
        functools.partial(relay_kernel, places),
        out_shape=jax.ShapeDtypeStruct((heads, HEAD_DIM, HEAD_DIM), F32),
        in_specs=[vmem],
        out_specs=vmem,
        scratch_shapes=[
            pltpu.VMEM((heads, HEAD_DIM, HEAD_DIM), F32),
            pltpu.VMEM((heads, HEAD_DIM, HEAD_DIM), F32),
            pltpu.SemaphoreType.DMA((heads,)),
            pltpu.SemaphoreType.DMA((heads,)),
        ],
        compiler_params=pltpu.CompilerParams(
            collective_id=0, has_side_effects=True, vmem_limit_bytes=32 * 1024 * 1024
        ),
        name="relay",
    )(state)
    count = lax.axis_size("head")
    quarter = rows // count
    chunk = min(quarter, 128)
    chunks = quarter // chunk
    near = (count // 2, chunks)
    far = (max(count // 2 - 1, 1), chunks)
    return pl.pallas_call(
        functools.partial(emit_kernel, count),
        out_shape=jax.ShapeDtypeStruct((quarter, model), BF16),
        in_specs=[vmem] * 5,
        out_specs=vmem,
        scratch_shapes=[
            pltpu.VMEM((chunk, value_width), BF16),
            pltpu.VMEM(near + (chunk, model), F32),
            pltpu.VMEM(near + (chunk, model), F32),
            pltpu.VMEM(far + (chunk, model), jnp.int16),
            pltpu.VMEM(far + (chunk, model), jnp.int16),
            pltpu.VMEM(far + (8, 128), F32),
            pltpu.VMEM(far + (8, 128), F32),
        ]
        + [pltpu.SemaphoreType.DMA(near)] * 2
        + [pltpu.SemaphoreType.DMA(far)] * 4,
        compiler_params=pltpu.CompilerParams(
            collective_id=1, has_side_effects=True, vmem_limit_bytes=56 * 1024 * 1024
        ),
        name="emit_scatter",
    )(eb, gate_branch, incoming, norm_gain.reshape(1, HEAD_DIM), out_weight)


def solution(mesh):
    return jax.shard_map(
        shards,
        mesh=mesh,
        in_specs=(P("ctx", "head"),) * 6 + (P(None, "head"),) * 3 + (P(), P("head", None)),
        out_specs=P(("ctx", "head"), None),
        check_vma=False,
    )
```
